256 devices in a mesh: dp: 2 (over y_lo), row: 8 (over z), col: 16 (over y_hi, x, core).
Axes of the slice: x: 4, y: 4 (y_hi: 2, y_lo: 2; y = y_hi * 2 + y_lo), z: 8, core: 2. Of those that a mesh axis runs over, the one named last changes fastest.
Arguments:
- tokens_in: bfloat16 [2048, 6144], P(('dp', 'row'), 'col'), may hold values from -6 to 6
- w_in: bfloat16 [6144, 24576], P('col', 'row'), may hold values from -0.078125 to 0.078125
- bias_in: float32 [24576], P('row'), may hold values from -3 to 3
- upstream: bfloat16 [2048, 24576], P(('dp', 'col'), 'row'), may hold values from -6 to 6
Outputs:
- activated: bfloat16 [2048, 24576], P(('dp', 'col'), 'row')
- input_grad: bfloat16 [2048, 6144], P(('dp', 'row'), 'col')
- weight_grad: float32 [6144, 24576], P('col', 'row')
- bias_grad: float32 [24576], P('row')
The draws below stay inside these ranges and needn't reach their ends.
All inputs are finite; a program needn't handle non-finite values.
Results may differ from the reference program's by a relative error of at most 0.023.
Values may be sent and summed in bfloat16 or wider, within the bound.
No kernel may reach another device: no remote copies, remote signals or barrier semaphores. Data moves between devices by JAX's collectives and lax.ppermute only.
A program may use at most 128 MiB of HBM per device.

```python
import jax
import jax.numpy as jnp
from jax import lax

D = 6144
F = 24576
TOKENS = 2048


def with_spikes(drawn, own_key, source, target, parts, factor):
    owner, partner = [(jnp.arange(drawn.shape[dim]) // (drawn.shape[dim] // parts)).reshape([-1 if axis == dim else 1 for axis in range(drawn.ndim)]) for dim in (source, target)]
    chosen = jax.random.permutation(own_key, parts)[partner]
    strong = (owner == chosen) | (owner == (partner + parts // 2) % parts)
    return jnp.where(strong, factor * drawn, drawn)


def level_of(stream_key, dims, cuts, least, top_value):
    def one(axis_at, blocks):
        draws = jax.random.uniform(jax.random.fold_in(jax.random.fold_in(stream_key, 6), axis_at), (blocks,), jnp.float32, least / len(cuts), top_value / len(cuts))
        return jnp.repeat(jnp.exp(draws), dims[axis_at] // blocks).reshape((-1,) + (1,) * (len(dims) - axis_at - 1))

    factor_of = one(*cuts[0])
    for cut in cuts[1:]:
        factor_of = factor_of * one(*cut)
    return factor_of


def gaussian(rng, shape, spread, bound, shards=(), held_as=jnp.bfloat16):
    result = jax.random.normal(rng, shape, jnp.float32) * spread
    if len(shards) > 0:
        result = level_of(rng, shape, shards, -0.22, 0.18) * result
    return jnp.clip(result, min=-bound, max=bound).astype(held_as)


def bell_draw_with(stream_key, shape, deviation, most, shards, heavy, kind=jnp.bfloat16):
    array = deviation * jax.random.normal(stream_key, shape, jnp.float32)
    if shards:
        array = array * level_of(stream_key, shape, shards, -0.22, 0.18)
    return jnp.clip(with_spikes(array, jax.random.fold_in(stream_key, 3), *heavy), -most, most).astype(kind)


def setup_inputs(seed: int = 0) -> dict:
    key_of = jax.random.split(jax.random.key(seed), 5)
    return {
        "tokens_in": bell_draw_with(key_of[0], (TOKENS, D), 1.0, 6.0, ((0, 16), (1, 16)), (1, 0, 16, 2.0)),
        "w_in": gaussian(key_of[1], (D, F), D ** -0.5, 0.078125, ((0, 16), (1, 8))),
        "bias_in": gaussian(key_of[2], (F,), 0.5, 3.0, ((0, 8),), jnp.float32),
        "upstream": bell_draw_with(key_of[3], (TOKENS, F), 1.0, 6.0, ((0, 32), (1, 8)), (1, 0, 32, 2.75)),
    }


def gelu_exact(value):
    return jax.nn.gelu(value, approximate=False)

def reference(tokens_in, w_in, bias_in, upstream):
    pre = jnp.dot(tokens_in, w_in, preferred_element_type=jnp.float32) + bias_in[None, :]
    activated_full, pullback = jax.vjp(gelu_exact, pre)
    activated = activated_full.astype(jnp.bfloat16)
    hidden_grad = pullback(upstream.astype(jnp.float32))[0].astype(jnp.bfloat16)
    input_grad = jnp.dot(hidden_grad, w_in.T, preferred_element_type=jnp.float32).astype(jnp.bfloat16)
    scale = 1.0 / jnp.sqrt(jnp.float32(TOKENS))
    weight_grad = jnp.dot(tokens_in.T, hidden_grad, preferred_element_type=jnp.float32) * scale
    bias_grad = lax.optimization_barrier(jnp.sum(hidden_grad.astype(jnp.float32), axis=0)) * scale
    return (activated, input_grad, weight_grad, bias_grad)
```

```python
import jax
import jax.numpy as jnp
from jax import lax
from jax.sharding import PartitionSpec as P

CHUNKS = 4
BF16 = jnp.bfloat16
F32 = jnp.float32


def gelu_exact(value):
    return jax.nn.gelu(value, approximate=False)


def col_index(hi, x, core):
    return ((hi % 2) * 4 + x % 4) * 2 + core % 2


PLACES = [(h, x, c) for h in range(2) for x in range(4) for c in range(2)]
CORE = [(col_index(h, x, c), col_index(h, x, c + 1)) for h, x, c in PLACES]
HIGH = [(col_index(h, x, c), col_index(h + 1, x, c)) for h, x, c in PLACES]
RIGHT = [(col_index(h, x, c), col_index(h, x + 1, c)) for h, x, c in PLACES]
LEFT = [(col_index(h, x, c), col_index(h, x - 1, c)) for h, x, c in PLACES]
PAIR = [(col_index(h, x, c), col_index(h, x ^ 1, c)) for h, x, c in PLACES]
FAR = [(col_index(h, x, c), col_index(h, x ^ 2, c)) for h, x, c in PLACES]
UP = [(i, (i + 1) % 8) for i in range(8)]
DOWN = [(i, (i - 1) % 8) for i in range(8)]
SWAP = [(0, 1), (1, 0)]


def matmul(a, b, dims):
    return lax.dot_general(a, b, ((dims[:1], dims[1:]), ((), ())), preferred_element_type=F32)


def add(*parts):
    total = parts[0].astype(F32)
    for part in parts[1:]:
        total = total + part.astype(F32)
    return total


def gather_rows(block):
    blocks = [None] * 8
    blocks[0] = block
    from_below = from_above = block
    for step in range(1, 4):
        from_below = lax.ppermute(from_below, "row", UP)
        from_above = lax.ppermute(from_above, "row", DOWN)
        blocks[-step] = from_below
        blocks[step] = from_above
    half = block.shape[0] // 2
    blocks[4] = jnp.concatenate(
        [
            lax.ppermute(from_below[:half], "row", UP),
            lax.ppermute(from_above[half:], "row", DOWN),
        ]
    )
    return blocks


def scatter_rows(blocks):
    half = blocks[4].shape[0] // 2
    far = blocks[4].astype(BF16)
    up = lax.ppermute(far[:half], "row", UP)
    down = lax.ppermute(far[half:], "row", DOWN)
    head = jnp.concatenate([add(blocks[3][:half], up), blocks[3][half:]]).astype(BF16)
    tail = jnp.concatenate([blocks[5][:half], add(blocks[5][half:], down)]).astype(BF16)
    for step in (2, 1):
        up = lax.ppermute(head, "row", UP)
        down = lax.ppermute(tail, "row", DOWN)
        head = add(blocks[step], up).astype(BF16)
        tail = add(blocks[8 - step], down).astype(BF16)
    return add(blocks[0], lax.ppermute(head, "row", UP), lax.ppermute(tail, "row", DOWN)).astype(BF16)


def body(tokens_in, w_in, bias_in, upstream):
    row = lax.axis_index("row")
    col = lax.axis_index("col")
    hi, x, core = col // 8, (col // 2) % 4, col % 2
    features, hidden = w_in.shape
    size = hidden // CHUNKS
    rows = upstream.shape[0]

    places = [(dc, dx, dh) for dc in range(2) for dx in range(4) for dh in range(2)]
    stacked = jnp.stack(gather_rows(tokens_in)).reshape(16, rows, features)

    def token_place(dc, dx, dh):
        block = jnp.bitwise_xor(hi, dh) * 4 + (x + dx) % 4
        return ((block - row) % 8) * 2 + jnp.bitwise_xor(core, dc)

    tokens = jnp.concatenate(
        [lax.dynamic_index_in_dim(stacked, token_place(*place), 0, keepdims=False) for place in places]
    )
    kept, given = tokens[: 8 * rows], tokens[8 * rows :]

    def forward(k):
        weights = w_in[:, k * size : (k + 1) * size]
        other = lax.ppermute(matmul(given, weights, (1, 0)).astype(BF16), "col", CORE)
        part = add(matmul(kept, weights, (1, 0)), other).astype(BF16)
        part = part.reshape(4, 2, rows, size)
        right = lax.ppermute(part[2, 0], "col", RIGHT)
        left = lax.ppermute(part[2, 1], "col", LEFT)
        to_right = jnp.stack([add(part[1, 0], right).astype(BF16), part[1, 1]])
        to_left = jnp.stack([part[3, 0], add(part[3, 1], left).astype(BF16)])
        right = lax.ppermute(to_right, "col", RIGHT)
        left = lax.ppermute(to_left, "col", LEFT)
        part = add(part[0], right, left)
        pre = part[0] + lax.ppermute(part[1].astype(BF16), "col", HIGH).astype(F32)
        pre = pre + bias_in[None, k * size : (k + 1) * size]
        activated, pullback = jax.vjp(gelu_exact, pre)
        grad = pullback(upstream[:, k * size : (k + 1) * size].astype(F32))[0].astype(BF16)
        return activated.astype(BF16), grad

    def backward(k, grad):
        weights = w_in[:, k * size : (k + 1) * size]
        own = jnp.stack([grad, lax.ppermute(grad, "col", HIGH)])
        from_left = lax.ppermute(own, "col", RIGHT)
        from_right = lax.ppermute(own, "col", LEFT)
        far = jnp.stack(
            [
                lax.ppermute(from_left[0], "col", RIGHT),
                lax.ppermute(from_right[1], "col", LEFT),
            ]
        )
        half = jnp.concatenate([own, from_right, far, from_left]).reshape(8 * rows, size)
        full = jnp.concatenate([half, lax.ppermute(half, "col", CORE)])
        weight_part = lax.optimization_barrier(matmul(tokens, full, (0, 0)).astype(BF16))
        other = lax.ppermute(weight_part, "dp", SWAP)
        return weight_part, other, matmul(full, weights, (1, 1))

    grads = [forward(k) for k in range(CHUNKS)]
    activated = jnp.concatenate([g[0] for g in grads], axis=1)
    hidden_grads = [g[1] for g in grads]

    bias_sum = jnp.sum(jnp.concatenate(hidden_grads, axis=1).astype(F32), axis=0)
    for axis, pairs in (("col", CORE), ("col", PAIR), ("col", FAR), ("col", HIGH), ("dp", SWAP)):
        bias_sum = bias_sum + lax.ppermute(bias_sum, axis, pairs)

    parts = [backward(k, hidden_grads[k]) for k in range(CHUNKS)]
    scale = 1.0 / jnp.sqrt(F32(2 * 16 * rows))
    weight_grad = jnp.concatenate([add(p[0], p[1]) * scale for p in parts], axis=1)

    input_part = parts[0][2]
    for p in parts[1:]:
        input_part = input_part + p[2]
    input_part = input_part.reshape(16, rows, features)

    def grad_place(k, a):
        block = (row + k) % 8
        dh = jnp.bitwise_xor(block // 4, hi)
        dx = (block % 4 - x) % 4
        return (jnp.bitwise_xor(core, a) * 4 + dx) * 2 + dh

    blocks = [
        jnp.concatenate(
            [lax.dynamic_index_in_dim(input_part, grad_place(k, a), 0, keepdims=False) for a in range(2)]
        )
        for k in range(8)
    ]
    input_grad = scatter_rows(blocks)
    return (activated, input_grad, weight_grad, bias_sum * scale)


def solution(mesh):
    return jax.shard_map(
        body,
        mesh=mesh,
        in_specs=(P(("dp", "row"), "col"), P("col", "row"), P("row"), P(("dp", "col"), "row")),
        out_specs=(P(("dp", "col"), "row"), P(("dp", "row"), "col"), P("col", "row"), P("row")),
        check_vma=False,
    )
```

```python
import jax
import jax.numpy as jnp
from jax import lax
from jax.experimental import pallas as pl
from jax.experimental.pallas import tpu as pltpu
from jax.sharding import PartitionSpec as P

CHUNKS = 3
EARLY = 1
BF16 = jnp.bfloat16
F32 = jnp.float32
ORDERS = {
    3: (
        ("2", 0),
        ("2", 1),
        ("2", 2),
        ("y", 0),
        ("y", 1),
        ("g", 0),
        ("y", 2),
        ("g", 1),
        ("f", 0),
        ("g", 2),
        ("f", 1),
        ("p", 0),
        ("f", 2),
        ("p", 1),
        ("p", 2),
    ),
    4: (
        ("2", 0),
        ("2", 1),
        ("y", 0),
        ("2", 2),
        ("2", 3),
        ("y", 1),
        ("g", 0),
        ("y", 2),
        ("g", 1),
        ("f", 0),
        ("y", 3),
        ("g", 2),
        ("f", 1),
        ("p", 0),
        ("g", 3),
        ("f", 2),
        ("p", 1),
        ("f", 3),
        ("p", 2),
        ("p", 3),
    ),
}


def gelu_exact(value):
    return jax.nn.gelu(value, approximate=False)


def col_index(hi, x, core):
    return ((hi % 2) * 4 + x % 4) * 2 + core % 2


PLACES = [(h, x, c) for h in range(2) for x in range(4) for c in range(2)]
CORE = [(col_index(h, x, c), col_index(h, x, c + 1)) for h, x, c in PLACES]
HIGH = [(col_index(h, x, c), col_index(h + 1, x, c)) for h, x, c in PLACES]
HIGH_ODD = [(col_index(h, x, 1), col_index(h + 1, x, 1)) for h, x, c in PLACES if c == 1]
ALONG_X = [(col_index(h, x, c), col_index(h, x + 1 - 2 * c, c)) for h, x, c in PLACES]
REPLICA = [
    (d * 16 + col_index(h, x, c), (1 - d) * 16 + col_index(h + c, x, c))
    for d in range(2)
    for h, x, c in PLACES
]
SWAP = [(0, 1), (1, 0)]
ORDER_OUT = [(1, 0), (1, 1), (2, 0), (0, 0), (3, 1), (3, 0), (2, 1), (0, 1)]
ORDER_BACK = [(0, 0), (0, 1), (3, 0), (3, 1), (2, 0), (1, 1), (1, 0), (2, 1)]


def matmul(a, b, dims):
    return lax.dot_general(a, b, ((dims[:1], dims[1:]), ((), ())), preferred_element_type=F32)


def add(*parts):
    total = parts[0].astype(F32)
    for part in parts[1:]:
        total = total + part.astype(F32)
    return total


def swap_core(a):
    return lax.ppermute(a, "col", CORE)


def along_x(a):
    return lax.ppermute(a, "col", ALONG_X)


def after(a, b):
    return lax.optimization_barrier((a, b))


def reorder(spots, first, second, out):
    for at in range(out.shape[0]):
        out[at] = (first[spots[at]] + second[spots[at]]).astype(out.dtype)


def body(tokens_in, w_in, bias_in, upstream):
    col = lax.axis_index("col")
    hi, x, core = col // 8, (col // 2) % 4, col % 2
    features, hidden = w_in.shape
    size = hidden // CHUNKS
    rows = upstream.shape[0]
    pair = 2 * rows
    is_low = hi == 0

    def in_order(own, theirs):
        return jnp.concatenate([jnp.where(is_low, own, theirs), jnp.where(is_low, theirs, own)])

    upstream_both = in_order(upstream, lax.ppermute(upstream, "col", HIGH))

    stacked = lax.all_to_all(
        jnp.broadcast_to(tokens_in[None], (8,) + tokens_in.shape), "row", 0, 0, tiled=True
    ).reshape(16, rows, features)

    def ahead_of(value):
        return jnp.where(core == 0, value, -value)

    def arrange(order):
        pieces = []
        for ahead, other in order:
            for h in range(2):
                place = (h * 4 + (x + ahead_of(ahead)) % 4) * 2 + jnp.bitwise_xor(core, other)
                pieces.append(lax.dynamic_index_in_dim(stacked, place, 0, keepdims=False))
        return jnp.concatenate(pieces)

    def spot_of(h, xx, c):
        ahead, other = ahead_of(xx - x) % 4, jnp.bitwise_xor(core, c)
        spot = jnp.zeros((), jnp.int32)
        for at, (a, o) in enumerate(ORDER_BACK):
            spot = jnp.where((ahead == a) & (other == o), at, spot)
        return spot * 2 + h

    spots = [spot_of(h, xx, c) for h in range(2) for xx in range(4) for c in range(2)]

    tokens_out = arrange(ORDER_OUT)
    kept, given = tokens_out[: 4 * pair], tokens_out[4 * pair :]
    tokens = arrange(ORDER_BACK)
    sent_tokens = jnp.where(core == 0, tokens, lax.ppermute(tokens, "col", HIGH_ODD))

    token_sets = jnp.concatenate([tokens, sent_tokens], axis=1)
    columns = [slice(k * size, (k + 1) * size) for k in range(CHUNKS)]
    weights = [w_in[:, c] for c in columns]
    scale = 1.0 / jnp.sqrt(F32(2 * 16 * rows))

    parts, got, activated, grads, own = [], {}, [None] * CHUNKS, {}, {}
    for k in range(CHUNKS):
        other = swap_core(matmul(given, weights[k], (1, 0)).astype(BF16))
        part = add(matmul(kept, weights[k], (1, 0)), other).astype(BF16)
        parts.append(part)
        got["first", k] = along_x(part[2 * pair : 3 * pair])

    waiting = []

    def leave(out, send):
        waiting.append((out, send))

    def settle(data=None):
        while waiting:
            out, send = waiting.pop()
            if data is not None:
                out, data = after(out, data)
            send(out)
        return data

    def keep(name, k, move):
        def send(out):
            got[name, k] = move(out)

        return send

    def step_second(k):
        part = settle(parts[k][: 2 * pair])
        moved = jnp.concatenate([add(part[:pair], got["first", k]).astype(BF16), part[pair:]])
        leave(moved, keep("second", k, along_x))

    def step_far_y(k):
        part = settle(parts[k][3 * pair :])
        arrived = got["second", k]
        total = add(part, arrived[:pair], swap_core(arrived[pair:])).astype(BF16)
        total = lax.optimization_barrier(total)
        own[k] = total
        leave(total, keep("far_y", k, lambda out: lax.ppermute(out, "col", HIGH)))

    def step_gelu(k):
        cotangent = settle(upstream_both[:, columns[k]])
        pre = add(own[k], got["far_y", k]) + bias_in[None, columns[k]]
        value, pullback = jax.vjp(gelu_exact, pre)
        grad = pullback(cotangent.astype(F32))[0].astype(BF16)
        activated[k] = jnp.where(is_low, value[:rows], value[rows:]).astype(BF16)
        grads[k] = jnp.concatenate([grad, swap_core(grad)])
        leave(grads[k], keep("behind", k, along_x))

    def step_far_x(k):
        settle()
        leave(got["behind", k][:pair], keep("far", k, along_x))

    bias_parts, ends = [None] * CHUNKS, {}
    input_sum = []

    full = {}

    def products(k, sets):
        both = lax.optimization_barrier(matmul(sets, full[k], (0, 0)).astype(BF16))
        got["replica", k] = lax.ppermute(both[features:], ("dp", "col"), REPLICA)
        ends[k] = both[:features]

    def step_products(k):
        sets = settle(token_sets)
        half = jnp.concatenate([got["behind", k], got["far", k]])
        full[k] = jnp.concatenate([grads[k], half, swap_core(half)])
        if k < EARLY:
            products(k, sets)
        input_sum.append(matmul(full[k], weights[k], (1, 1)))
        sums = jnp.sum(full[k].reshape(16, rows, size).astype(F32), axis=1)
        bias_part = jnp.zeros((1, size), F32)
        for spot in spots:
            bias_part = bias_part + lax.dynamic_slice_in_dim(sums, spot, 1, 0)
        bias_parts[k] = bias_part

    steps = {"2": step_second, "y": step_far_y, "g": step_gelu, "f": step_far_x, "p": step_products}
    for name, chunk in ORDERS[CHUNKS]:
        steps[name](chunk)
    settle()

    input_part = input_sum[0]
    for term in input_sum[1:-1]:
        input_part = input_part + term
    terms = pl.pallas_call(
        reorder,
        out_shape=jax.ShapeDtypeStruct((16, rows, features), BF16),
        in_specs=[
            pl.BlockSpec(memory_space=pltpu.SMEM),
            pl.BlockSpec(memory_space=pltpu.VMEM),
            pl.BlockSpec(memory_space=pltpu.VMEM),
        ],
        out_specs=pl.BlockSpec(memory_space=pltpu.VMEM),
        cost_estimate=pl.CostEstimate(flops=1 << 19, bytes_accessed=4 << 20, transcendentals=0),
    )(
        jnp.stack(spots).astype(jnp.int32),
        input_part.reshape(16, rows, features),
        input_sum[-1].reshape(16, rows, features),
    )
    terms, late_sets = after(terms, token_sets)
    terms = lax.all_to_all(terms.reshape(8, pair, features), "row", 0, 0, tiled=True)
    input_grad = jnp.sum(terms.astype(F32), axis=0).astype(BF16)

    for k in range(EARLY, CHUNKS):
        products(k, late_sets)
    bias_own = jnp.concatenate(bias_parts, axis=1).astype(BF16).reshape(-1, 128)
    bias_own = lax.optimization_barrier(bias_own)
    bias_grad = add(bias_own, lax.ppermute(bias_own, "dp", SWAP)).reshape(hidden) * scale

    result = jnp.concatenate([add(ends[k], got["replica", k]) * scale for k in range(CHUNKS)], axis=1)
    return (jnp.concatenate(activated, axis=1), input_grad, result, bias_grad)


def solution(mesh):
    return jax.shard_map(
        body,
        mesh=mesh,
        in_specs=(P(("dp", "row"), "col"), P("col", "row"), P("row"), P(("dp", "col"), "row")),
        out_specs=(P(("dp", "col"), "row"), P(("dp", "row"), "col"), P("col", "row"), P("row")),
        check_vma=False,
    )
```

```python
import jax
import jax.numpy as jnp
from jax import lax
from jax.experimental import pallas as pl
from jax.experimental.pallas import tpu as pltpu
from jax.sharding import PartitionSpec as P

CHUNKS = 3
EARLY = 2
BF16 = jnp.bfloat16
F32 = jnp.float32
ORDERS = {
    3: (
        ("2", 0),
        ("2", 1),
        ("2", 2),
        ("y", 0),
        ("y", 1),
        ("g", 0),
        ("y", 2),
        ("g", 1),
        ("f", 0),
        ("g", 2),
        ("f", 1),
        ("p", 0),
        ("f", 2),
        ("p", 1),
        ("p", 2),
    ),
    4: (
        ("2", 0),
        ("2", 1),
        ("y", 0),
        ("2", 2),
        ("2", 3),
        ("y", 1),
        ("g", 0),
        ("y", 2),
        ("g", 1),
        ("f", 0),
        ("y", 3),
        ("g", 2),
        ("f", 1),
        ("p", 0),
        ("g", 3),
        ("f", 2),
        ("p", 1),
        ("f", 3),
        ("p", 2),
        ("p", 3),
    ),
}


def gelu_exact(value):
    return jax.nn.gelu(value, approximate=False)


def col_index(hi, x, core):
    return ((hi % 2) * 4 + x % 4) * 2 + core % 2


PLACES = [(h, x, c) for h in range(2) for x in range(4) for c in range(2)]
CORE = [(col_index(h, x, c), col_index(h, x, c + 1)) for h, x, c in PLACES]
HIGH = [(col_index(h, x, c), col_index(h + 1, x, c)) for h, x, c in PLACES]
HIGH_ODD = [(col_index(h, x, 1), col_index(h + 1, x, 1)) for h, x, c in PLACES if c == 1]
ALONG_X = [(col_index(h, x, c), col_index(h, x + 1 - 2 * c, c)) for h, x, c in PLACES]
REPLICA = [
    (d * 16 + col_index(h, x, c), (1 - d) * 16 + col_index(h + c, x, c))
    for d in range(2)
    for h, x, c in PLACES
]
SWAP = [(0, 1), (1, 0)]
ORDER_OUT = [(1, 0), (1, 1), (2, 0), (0, 0), (3, 1), (3, 0), (2, 1), (0, 1)]
ORDER_BACK = [(0, 0), (0, 1), (3, 0), (3, 1), (2, 0), (1, 1), (1, 0), (2, 1)]


def matmul(a, b, dims):
    return lax.dot_general(a, b, ((dims[:1], dims[1:]), ((), ())), preferred_element_type=F32)


def add(*parts):
    total = parts[0].astype(F32)
    for part in parts[1:]:
        total = total + part.astype(F32)
    return total


def swap_core(a):
    return lax.ppermute(a, "col", CORE)


def along_x(a):
    return lax.ppermute(a, "col", ALONG_X)


def after(a, b):
    return lax.optimization_barrier((a, b))


def reorder(spots, first, second, out):
    for at in range(out.shape[0]):
        out[at] = (first[spots[at]] + second[spots[at]]).astype(out.dtype)


def body(tokens_in, w_in, bias_in, upstream):
    col = lax.axis_index("col")
    hi, x, core = col // 8, (col // 2) % 4, col % 2
    features, hidden = w_in.shape
    size = hidden // CHUNKS
    rows = upstream.shape[0]
    pair = 2 * rows
    is_low = hi == 0

    def in_order(own, theirs):
        return jnp.concatenate([jnp.where(is_low, own, theirs), jnp.where(is_low, theirs, own)])

    upstream_both = in_order(upstream, lax.ppermute(upstream, "col", HIGH))

    stacked = lax.all_to_all(
        jnp.broadcast_to(tokens_in[None], (8,) + tokens_in.shape), "row", 0, 0, tiled=True
    ).reshape(16, rows, features)

    def ahead_of(value):
        return jnp.where(core == 0, value, -value)

    def arrange(order):
        pieces = []
        for ahead, other in order:
            for h in range(2):
                place = (h * 4 + (x + ahead_of(ahead)) % 4) * 2 + jnp.bitwise_xor(core, other)
                pieces.append(lax.dynamic_index_in_dim(stacked, place, 0, keepdims=False))
        return jnp.concatenate(pieces)

    def spot_of(h, xx, c):
        ahead, other = ahead_of(xx - x) % 4, jnp.bitwise_xor(core, c)
        spot = jnp.zeros((), jnp.int32)
        for at, (a, o) in enumerate(ORDER_BACK):
            spot = jnp.where((ahead == a) & (other == o), at, spot)
        return spot * 2 + h

    spots = [spot_of(h, xx, c) for h in range(2) for xx in range(4) for c in range(2)]

    tokens_out = arrange(ORDER_OUT)
    kept, given = tokens_out[: 4 * pair], tokens_out[4 * pair :]
    tokens = arrange(ORDER_BACK)
    sent_tokens = jnp.where(core == 0, tokens, lax.ppermute(tokens, "col", HIGH_ODD))

    token_sets = jnp.concatenate([tokens, sent_tokens], axis=1)
    columns = [slice(k * size, (k + 1) * size) for k in range(CHUNKS)]
    weights = [w_in[:, c] for c in columns]
    scale = 1.0 / jnp.sqrt(F32(2 * 16 * rows))

    parts, got, activated, grads, own = [], {}, [None] * CHUNKS, {}, {}
    for k in range(CHUNKS):
        other = swap_core(matmul(given, weights[k], (1, 0)).astype(BF16))
        part = add(matmul(kept, weights[k], (1, 0)), other).astype(BF16)
        parts.append(part)
        got["first", k] = along_x(part[2 * pair : 3 * pair])

    waiting = []

    def leave(out, send):
        waiting.append((out, send))

    def settle(data=None):
        while waiting:
            out, send = waiting.pop()
            if data is not None:
                out, data = after(out, data)
            send(out)
        return data

    def keep(name, k, move):
        def send(out):
            got[name, k] = move(out)

        return send

    def step_second(k):
        part = settle(parts[k][: 2 * pair])
        moved = jnp.concatenate([add(part[:pair], got["first", k]).astype(BF16), part[pair:]])
        leave(moved, keep("second", k, along_x))

    def step_far_y(k):
        part = settle(parts[k][3 * pair :])
        arrived = got["second", k]
        total = add(part, arrived[:pair], swap_core(arrived[pair:])).astype(BF16)
        total = lax.optimization_barrier(total)
        own[k] = total
        leave(total, keep("far_y", k, lambda out: lax.ppermute(out, "col", HIGH)))

    def step_gelu(k):
        cotangent = settle(upstream_both[:, columns[k]])
        pre = add(own[k], got["far_y", k]) + bias_in[None, columns[k]]
        value, pullback = jax.vjp(gelu_exact, pre)
        grad = pullback(cotangent.astype(F32))[0].astype(BF16)
        activated[k] = jnp.where(is_low, value[:rows], value[rows:]).astype(BF16)
        grads[k] = jnp.concatenate([grad, swap_core(grad)])
        leave(grads[k], keep("behind", k, along_x))

    def step_far_x(k):
        settle()
        leave(got["behind", k][:pair], keep("far", k, along_x))

    bias_parts, ends = [None] * CHUNKS, {}
    input_sum = []

    full = {}

    def products(k, sets):
        both = lax.optimization_barrier(matmul(sets, full[k], (0, 0)).astype(BF16))
        got["replica", k] = lax.ppermute(both[features:], ("dp", "col"), REPLICA)
        ends[k] = both[:features]

    def step_products(k):
        sets = settle(token_sets)
        half = jnp.concatenate([got["behind", k], got["far", k]])
        full[k] = jnp.concatenate([grads[k], half, swap_core(half)])
        if k < EARLY:
            products(k, sets)
        part_weights = weights[k]
        if k == CHUNKS - 1:
            for early in range(EARLY):
                ends[early], part_weights = after(ends[early], part_weights)
        input_sum.append(matmul(full[k], part_weights, (1, 1)))
        sums = jnp.sum(full[k].reshape(16, rows, size).astype(F32), axis=1)
        bias_part = jnp.zeros((1, size), F32)
        for spot in spots:
            bias_part = bias_part + lax.dynamic_slice_in_dim(sums, spot, 1, 0)
        bias_parts[k] = bias_part

    steps = {"2": step_second, "y": step_far_y, "g": step_gelu, "f": step_far_x, "p": step_products}
    for name, chunk in ORDERS[CHUNKS]:
        steps[name](chunk)
    settle()

    input_part = input_sum[0]
    for term in input_sum[1:-1]:
        input_part = input_part + term
    terms = pl.pallas_call(
        reorder,
        out_shape=jax.ShapeDtypeStruct((16, rows, features), BF16),
        in_specs=[
            pl.BlockSpec(memory_space=pltpu.SMEM),
            pl.BlockSpec(memory_space=pltpu.VMEM),
            pl.BlockSpec(memory_space=pltpu.VMEM),
        ],
        out_specs=pl.BlockSpec(memory_space=pltpu.VMEM),
        cost_estimate=pl.CostEstimate(flops=1 << 19, bytes_accessed=4 << 20, transcendentals=0),
    )(
        jnp.stack(spots).astype(jnp.int32),
        input_part.reshape(16, rows, features),
        input_sum[-1].reshape(16, rows, features),
    )
    bias_own = jnp.concatenate(bias_parts, axis=1).astype(BF16).reshape(-1, 128)
    bias_own, terms = after(bias_own, terms)
    bias_other, late_sets = after(lax.ppermute(bias_own, "dp", SWAP), token_sets)
    bias_grad = add(bias_own, bias_other).reshape(hidden) * scale

    terms = lax.all_to_all(terms.reshape(8, pair, features), "row", 0, 0, tiled=True)
    input_grad = jnp.sum(terms.astype(F32), axis=0).astype(BF16)

    for k in range(EARLY, CHUNKS):
        products(k, late_sets)
    result = jnp.concatenate([add(ends[k], got["replica", k]) * scale for k in range(CHUNKS)], axis=1)
    return (jnp.concatenate(activated, axis=1), input_grad, result, bias_grad)


def solution(mesh):
    return jax.shard_map(
        body,
        mesh=mesh,
        in_specs=(P(("dp", "row"), "col"), P("col", "row"), P("row"), P(("dp", "col"), "row")),
        out_specs=(P(("dp", "col"), "row"), P(("dp", "row"), "col"), P("col", "row"), P("row")),
        check_vma=False,
    )
```
